32 devices in a mesh: chan: 8 (over z, y), hour: 4 (over x, core).
Axes of the slice: x: 2, y: 2, z: 4, core: 2. Of those that a mesh axis runs over, the one named last changes fastest.
Arguments:
- records: bfloat16 [320, 64, 2048], P('chan', 'hour'), may hold values from -6 to 6
- live_channels: int32 [320], P('chan'), may hold values 0 or 1
- live_windows: int32 [64], P('hour'), may hold values 0 or 1
Outputs:
- correlations: bfloat16 [320, 2, 40, 512], P('chan', None, None, 'hour')
The draws below stay inside these ranges and needn't reach their ends.
All inputs are finite; a program needn't handle non-finite values. No bound on the sum of `live_channels` or of `live_windows` on one device may be relied on, other than what follows from the above.
Results may differ from the reference program's by a relative error of at most 0.013.
Values may be sent and summed in bfloat16 or wider, within the bound.
A program may use at most 128 MiB of HBM per device.

```python
import math
import jax
import jax.numpy as jnp
from jax import lax

BLOCK = 40
SAMPLES = 2048
BAND = 512
FIRST_BIN = 32
HALF = 64
LAGS = 512
NSHIFT = 2
W_DEV = 16
CHANNELS = 320
WINDOWS = 64
N_CHAN = 8
N_HOUR = 4


def with_ends(values, key, smallest, top_value):
    index_at = [jax.random.randint(jax.random.fold_in(key, axis), (), 0, length) for axis, length in enumerate(values.shape)]
    longest = values.shape.index(max(values.shape))
    neighbour = index_at[:longest] + [(index_at[longest] + 1) % values.shape[longest]] + index_at[longest + 1:]
    return values.at[tuple(index_at)].set(smallest).at[tuple(neighbour)].set(top_value)


def levels(stream_key, dims, cuts, least, top_value):
    loudness, own = 1.0, jax.random.fold_in(stream_key, 6)
    for axis_at, blocks in cuts:
        steps = jnp.exp(jax.random.uniform(jax.random.fold_in(own, axis_at), (blocks,), jnp.float32, least / len(cuts), top_value / len(cuts)))
        loudness = loudness * jnp.repeat(steps, dims[axis_at] // blocks).reshape([-1 if axis == axis_at else 1 for axis in range(len(dims))])
    return loudness


def centred(rng, extent, width, reach, cuts=(), kind=jnp.bfloat16):
    values = width * jax.random.normal(rng, extent, jnp.float32)
    if cuts:
        values = values * levels(rng, extent, cuts, -0.22, 0.18)
    return jnp.clip(values, -reach, reach).astype(kind)


def setup_inputs(seed: int = 0) -> dict:
    streams_of = jax.random.split(jax.random.key(seed), 4)
    records = centred(streams_of[0], (CHANNELS, WINDOWS, SAMPLES), 1.0, 6.0, ((0, 8), (1, 4)))
    live_channels = with_ends((jax.random.randint(streams_of[1], (CHANNELS,), 0, 16) < 15).astype(jnp.int32), jax.random.fold_in(streams_of[1], 1), 0, 1)
    live_windows = with_ends((jax.random.randint(streams_of[2], (WINDOWS,), 0, 8) < 7).astype(jnp.int32), jax.random.fold_in(streams_of[2], 1), 0, 1)
    return {"records": records, "live_channels": live_channels, "live_windows": live_windows}


def forward_table():
    times = jnp.arange(SAMPLES, dtype=jnp.int32)[:, None]
    bins = FIRST_BIN + jnp.arange(BAND, dtype=jnp.int32)[None, :]
    phase = times * bins % SAMPLES
    angle = phase.astype(jnp.float32) * (2.0 * math.pi / SAMPLES)
    return jnp.concatenate([jnp.cos(angle), -jnp.sin(angle)], axis=1).astype(jnp.bfloat16)

def inverse_table():
    bins = FIRST_BIN + jnp.arange(BAND, dtype=jnp.int32)[:, None]
    shifts = jnp.arange(LAGS, dtype=jnp.int32)[None, :] - LAGS // 2
    phase = bins * shifts % SAMPLES
    angle = phase.astype(jnp.float32) * (2.0 * math.pi / SAMPLES)
    return jnp.concatenate([jnp.cos(angle), -jnp.sin(angle)], axis=0).astype(jnp.bfloat16)

def smoothing_matrix():
    index = jnp.arange(BAND, dtype=jnp.int32)
    inside = (jnp.abs(index[:, None] - index[None, :]) <= HALF).astype(jnp.float32)
    counts = lax.optimization_barrier(jnp.sum(inside, axis=0, keepdims=True))
    return inside / counts

def whiten(spectra, live_rows, smoother):
    real_part = spectra[:, :BAND]
    imag_part = spectra[:, BAND:]
    amplitude = jnp.sqrt(real_part * real_part + imag_part * imag_part)
    smooth = jnp.dot(amplitude, smoother, precision=lax.Precision.HIGHEST)
    factor = live_rows / (smooth + 1e-06)
    return jnp.concatenate([real_part * factor, imag_part * factor], axis=1).astype(jnp.bfloat16)

def cross_lags(own_spectra, other_spectra, inverse, norm_factor):
    own_real = own_spectra[..., :BAND].astype(jnp.float32)
    own_imag = own_spectra[..., BAND:].astype(jnp.float32)
    far_real = other_spectra[..., :BAND].astype(jnp.float32)
    far_imag = other_spectra[..., BAND:].astype(jnp.float32)

    def inner(left, right):
        return jnp.einsum('cwf,dwf->cdf', left, right)
    cross_real = inner(own_real, far_real) + inner(own_imag, far_imag)
    cross_imag = inner(own_real, far_imag) - inner(own_imag, far_real)
    stacked = jnp.concatenate([cross_real, cross_imag], axis=-1).astype(jnp.bfloat16)
    rows_here = stacked.shape[0] * stacked.shape[1]
    lagged = jnp.dot(stacked.reshape(rows_here, 2 * BAND).astype(jnp.float32), inverse.astype(jnp.float32))
    return (lagged * norm_factor).reshape(stacked.shape[0], stacked.shape[1], LAGS)

def reference(records, live_channels, live_windows):
    forward = forward_table().astype(jnp.float32)
    inverse = inverse_table()
    smoother = smoothing_matrix()
    norm_factor = 1.0 / math.sqrt(WINDOWS * BAND)
    window_live = live_windows.astype(jnp.float32)

    def spectra_of(operands):
        block_records, block_live = operands
        spectra = jnp.dot(block_records.reshape(BLOCK * WINDOWS, SAMPLES).astype(jnp.float32), forward)
        live_rows = (block_live.astype(jnp.float32)[:, None] * window_live[None, :]).reshape(BLOCK * WINDOWS, 1)
        return whiten(spectra, live_rows, smoother).reshape(BLOCK, WINDOWS, 2 * BAND)
    whitened = lax.map(spectra_of, (records.reshape(N_CHAN, BLOCK, WINDOWS, SAMPLES), live_channels.reshape(N_CHAN, BLOCK)))

    def correlate_block(block_index):
        own_spectra = whitened[block_index]

        def per_shift(shift_index):
            other_spectra = whitened[(block_index + shift_index + 1) % N_CHAN]

            def per_hour(hour_index):
                start = (hour_index * W_DEV).astype(jnp.int32)
                own_part = lax.dynamic_slice_in_dim(own_spectra, start, W_DEV, 1)
                far_part = lax.dynamic_slice_in_dim(other_spectra, start, W_DEV, 1)
                lagged = cross_lags(own_part, far_part, inverse, norm_factor)
                return lax.optimization_barrier(lagged.astype(jnp.bfloat16)).astype(jnp.float32)
            return lax.optimization_barrier(jnp.sum(lax.map(per_hour, jnp.arange(N_HOUR, dtype=jnp.int32)), axis=0))
        return lax.map(per_shift, jnp.arange(NSHIFT, dtype=jnp.int32))
    result = lax.map(correlate_block, jnp.arange(N_CHAN, dtype=jnp.int32))
    result = jnp.transpose(result, (0, 2, 1, 3, 4)).reshape(CHANNELS, NSHIFT, BLOCK, LAGS)
    return result.astype(jnp.bfloat16)
```

```python
import functools
import math

import jax
import jax.numpy as jnp
import ml_dtypes
import numpy as np
from jax import lax
from jax.experimental import pallas as pl
from jax.experimental.pallas import tpu as pltpu
from jax.sharding import PartitionSpec as P

SAMPLES = 2048
BAND = 512
FIRST_BIN = 32
HALF = 64
LAGS = 512
NSHIFT = 2
GROUP = 8
LANES = 128
MESH = pl.DeviceIdType.MESH


def forward_table():
    times = np.arange(SAMPLES)[:, None]
    bins = FIRST_BIN + np.arange(BAND)[None, :]
    angle = (times * bins % SAMPLES) * (2.0 * math.pi / SAMPLES)
    return np.concatenate([np.cos(angle), -np.sin(angle)], axis=1).astype(ml_dtypes.bfloat16)


def inverse_table():
    bins = FIRST_BIN + np.arange(BAND)[:, None]
    shifts = np.arange(LAGS)[None, :] - LAGS // 2
    angle = (bins * shifts % SAMPLES) * (2.0 * math.pi / SAMPLES)
    return np.concatenate([np.cos(angle), -np.sin(angle)], axis=0).astype(ml_dtypes.bfloat16)


def band_inside():
    index = np.arange(BAND)
    return np.abs(index[:, None] - index[None, :]) <= HALF


def kernel(
    n_chan, n_hour, channels, windows, norm_factor,
    records, live, forward, inside, weight, inverse, out,
    own, own_send, far_two, far_one, cross, lagged, heard, total,
    two_send, two_recv, one_send, one_recv, sum_send, sum_recv,
):
    chunks = channels // GROUP
    rows = GROUP * windows
    quarter = LAGS // n_hour
    me = lax.axis_index("chan")
    hour = lax.axis_index("hour")
    parity = lax.rem(me, 2)
    before = lax.rem(me + n_chan - 2, n_chan)
    after = lax.rem(me + 2, n_chan)
    twin = me + 1 - 2 * parity

    barrier = pltpu.get_barrier_semaphore()
    for chan in (before, after, twin):
        pl.semaphore_signal(barrier, inc=1, device_id=(chan, hour), device_id_type=MESH)
    for step in range(1, n_hour):
        other = lax.rem(hour + step, n_hour)
        pl.semaphore_signal(barrier, inc=1, device_id=(me, other), device_id_type=MESH)
    pl.semaphore_wait(barrier, 3 + n_hour - 1)

    def to_before(chunk):
        return pltpu.make_async_remote_copy(
            src_ref=own_send.at[chunk], dst_ref=far_two.at[chunk],
            send_sem=two_send.at[chunk], recv_sem=two_recv.at[chunk],
            device_id=(before, hour), device_id_type=MESH,
        )

    def to_twin(source, chunk):
        return pltpu.make_async_remote_copy(
            src_ref=source.at[chunk], dst_ref=far_one.at[chunk],
            send_sem=one_send.at[chunk], recv_sem=one_recv.at[chunk],
            device_id=(twin, hour), device_id_type=MESH,
        )

    def to_hour(step, distance):
        target = lax.rem(hour + distance, n_hour)
        return pltpu.make_async_remote_copy(
            src_ref=lagged.at[step, target], dst_ref=heard.at[step, distance - 1],
            send_sem=sum_send.at[step, distance - 1], recv_sem=sum_recv.at[step, distance - 1],
            device_id=(me, target), device_id_type=MESH,
        )

    def whiten_chunk(chunk, carry):
        start = pl.multiple_of(chunk * rows, rows)
        spectra = jnp.dot(
            records[pl.ds(start, rows), :], forward[...], preferred_element_type=jnp.float32
        )
        real_part = spectra[:, :BAND]
        imag_part = spectra[:, BAND:]
        amplitude = jnp.sqrt(real_part * real_part + imag_part * imag_part)
        high = amplitude.astype(jnp.bfloat16)
        low = (amplitude - high.astype(jnp.float32)).astype(jnp.bfloat16)
        smooth = jnp.dot(high, inside[...], preferred_element_type=jnp.float32)
        smooth = smooth + jnp.dot(low, inside[...], preferred_element_type=jnp.float32)
        factor = live[pl.ds(start, rows), :] / (smooth * weight[...] + 1e-06)
        for tile in range(BAND // LANES):
            at = slice(tile * LANES, (tile + 1) * LANES)
            for half, part in enumerate((real_part, imag_part)):
                value = (part[:, at] * factor[:, at]).astype(jnp.bfloat16).astype(jnp.float32)
                own[half * (BAND // LANES) + tile, pl.ds(start, rows), :] = value
        for tile in range(2 * BAND // LANES):
            for pair in range(windows // 2):
                both = [
                    own[tile, pl.ds(start + 2 * pair + part, GROUP, stride=windows), :]
                    for part in range(2)
                ]
                own_send[chunk, pl.ds(pair * 2 * GROUP, 2 * GROUP), pl.ds(tile * LANES, LANES)] = (
                    jnp.concatenate(both, axis=0).astype(jnp.bfloat16)
                )
        to_before(chunk).start()

        @pl.when(parity == 1)
        def _():
            to_twin(own_send, chunk).start()

        return carry

    lax.fori_loop(0, chunks, whiten_chunk, 0)

    def cross_lags(far, chunk, step):
        for tile in range(BAND // LANES):
            real_at = pl.ds(tile * LANES, LANES)
            imag_at = pl.ds(BAND + tile * LANES, LANES)
            far_real, far_imag = [], []
            for pair in range(windows // 2):
                at = pl.ds(pair * 2 * GROUP, 2 * GROUP)
                for lanes, parts in ((real_at, far_real), (imag_at, far_imag)):
                    both = far[chunk, at, lanes].astype(jnp.float32)
                    parts += [both[:GROUP], both[GROUP:]]

            def channel_pair(index, carry):
                reals, imags = [], []
                for part in range(2):
                    base = pl.multiple_of((2 * index + part) * windows, windows)
                    real = jnp.zeros((GROUP, LANES), jnp.float32)
                    imag = jnp.zeros((GROUP, LANES), jnp.float32)
                    for window in range(windows):
                        a_real = own[tile, pl.ds(base + window, GROUP, stride=0), :]
                        a_imag = own[BAND // LANES + tile, pl.ds(base + window, GROUP, stride=0), :]
                        real = real + a_real * far_real[window] + a_imag * far_imag[window]
                        imag = imag + a_real * far_imag[window] - a_imag * far_real[window]
                    reals.append(real)
                    imags.append(imag)
                at = pl.ds(pl.multiple_of(index * 2 * GROUP, 2 * GROUP), 2 * GROUP)
                cross[at, real_at] = jnp.concatenate(reals, axis=0).astype(jnp.bfloat16)
                cross[at, imag_at] = jnp.concatenate(imags, axis=0).astype(jnp.bfloat16)
                return carry

            lax.fori_loop(0, channels // 2, channel_pair, 0)
        result = jnp.dot(cross[...], inverse[...], preferred_element_type=jnp.float32) * norm_factor
        for part in range(n_hour):
            lagged[step, part] = result[:, part * quarter : (part + 1) * quarter].astype(jnp.bfloat16)
        for distance in range(1, n_hour):
            to_hour(step, distance).start()

    def correlate_chunk(chunk, carry):
        to_before(chunk).wait_recv()

        @pl.when(parity == 0)
        def _():
            to_twin(far_two, chunk).start()

        cross_lags(far_two, chunk, 2 * chunk + 1)
        to_twin(own_send, chunk).wait_recv()
        cross_lags(far_one, chunk, 2 * chunk)
        return carry

    lax.fori_loop(0, chunks, correlate_chunk, 0)

    def finish_chunk(chunk, carry):
        to_before(chunk).wait_send()
        to_twin(own_send, chunk).wait_send()
        for shift in range(NSHIFT):
            step = 2 * chunk + shift
            value = lagged[step, hour].astype(jnp.float32)
            for distance in range(1, n_hour):
                to_hour(step, distance).wait()
                value = value + heard[step, distance - 1].astype(jnp.float32)
            at = pl.ds(pl.multiple_of(chunk * GROUP, GROUP), GROUP)
            total[:, shift, at, :] = value.reshape(channels, GROUP, quarter)
        return carry

    lax.fori_loop(0, chunks, finish_chunk, 0)
    out[...] = total[...].astype(jnp.bfloat16)


def local(records, live_channels, live_windows):
    channels, windows, samples = records.shape
    n_chan, n_hour = lax.axis_size("chan"), lax.axis_size("hour")
    norm_factor = 1.0 / math.sqrt(windows * n_hour * BAND)
    chunks, rows, quarter = channels // GROUP, GROUP * windows, LAGS // n_hour
    steps = NSHIFT * chunks
    live = (
        live_channels.astype(jnp.float32)[:, None] * live_windows.astype(jnp.float32)[None, :]
    ).reshape(channels * windows, 1)
    inside = band_inside()
    weight = (1.0 / inside.sum(axis=0, keepdims=True)).astype(np.float32)
    whitened = pltpu.VMEM((chunks, rows, 2 * BAND), jnp.bfloat16)
    return pl.pallas_call(
        functools.partial(kernel, n_chan, n_hour, channels, windows, norm_factor),
        out_shape=jax.ShapeDtypeStruct((channels, NSHIFT, channels, quarter), jnp.bfloat16),
        in_specs=[pl.BlockSpec(memory_space=pltpu.VMEM)] * 6,
        out_specs=pl.BlockSpec(memory_space=pltpu.VMEM),
        scratch_shapes=[
            pltpu.VMEM((2 * BAND // LANES, channels * windows, LANES), jnp.float32),
            whitened,
            whitened,
            whitened,
            pltpu.VMEM((channels * GROUP, 2 * BAND), jnp.bfloat16),
            pltpu.VMEM((steps, n_hour, channels * GROUP, quarter), jnp.bfloat16),
            pltpu.VMEM((steps, n_hour - 1, channels * GROUP, quarter), jnp.bfloat16),
            pltpu.VMEM((channels, NSHIFT, channels, quarter), jnp.float32),
            pltpu.SemaphoreType.DMA((chunks,)),
            pltpu.SemaphoreType.DMA((chunks,)),
            pltpu.SemaphoreType.DMA((chunks,)),
            pltpu.SemaphoreType.DMA((chunks,)),
            pltpu.SemaphoreType.DMA((steps, n_hour - 1)),
            pltpu.SemaphoreType.DMA((steps, n_hour - 1)),
        ],
        compiler_params=pltpu.CompilerParams(
            collective_id=0, has_side_effects=True, vmem_limit_bytes=48 * 1024 * 1024
        ),
        name="correlate",
    )(
        records.reshape(channels * windows, samples),
        live,
        jnp.asarray(forward_table()),
        jnp.asarray(inside.astype(ml_dtypes.bfloat16)),
        jnp.asarray(weight),
        jnp.asarray(inverse_table()),
    )


def solution(mesh):
    placed = (P("chan", "hour", None), P("chan"), P("hour"))
    return jax.shard_map(
        local, mesh=mesh, in_specs=placed, out_specs=P("chan", None, None, "hour"), check_vma=False
    )
```

```python
import functools
import math

import jax
import jax.numpy as jnp
import ml_dtypes
import numpy as np
from jax import lax
from jax.experimental import pallas as pl
from jax.experimental.pallas import tpu as pltpu
from jax.sharding import PartitionSpec as P

SAMPLES = 2048
BAND = 512
FIRST_BIN = 32
HALF = 64
LAGS = 512
NSHIFT = 2
GROUP = 8
LANES = 128
MESH = pl.DeviceIdType.MESH


def forward_table():
    times = np.arange(SAMPLES)[:, None]
    bins = FIRST_BIN + np.arange(BAND)[None, :]
    angle = (times * bins % SAMPLES) * (2.0 * math.pi / SAMPLES)
    return np.concatenate([np.cos(angle), -np.sin(angle)], axis=1).astype(ml_dtypes.bfloat16)


def inverse_table():
    bins = FIRST_BIN + np.arange(BAND)[:, None]
    shifts = np.arange(LAGS)[None, :] - LAGS // 2
    angle = (bins * shifts % SAMPLES) * (2.0 * math.pi / SAMPLES)
    return np.concatenate([np.cos(angle), -np.sin(angle)], axis=0).astype(ml_dtypes.bfloat16)


def band_inside():
    index = np.arange(BAND)
    return np.abs(index[:, None] - index[None, :]) <= HALF


def kernel(
    n_chan, n_hour, channels, windows, norm_factor,
    records_hbm, channels_hbm, windows_hbm, forward_hbm, inside_hbm, weight_hbm, inverse_hbm, out,
    records, live_channels, live_windows, forward, inside, weight, inverse,
    own, own_send, far_two, far_one, far, cross, lagged, heard, total,
    load_sem, record_sem, two_send, two_recv, one_send, one_recv, sum_send, sum_recv,
):
    chunks = channels // GROUP
    rows = GROUP * windows
    quarter = LAGS // n_hour
    tiles = BAND // LANES
    me = lax.axis_index("chan")
    hour = lax.axis_index("hour")
    parity = lax.rem(me, 2)
    before = lax.rem(me + n_chan - 2, n_chan)
    after = lax.rem(me + 2, n_chan)
    twin = me + 1 - 2 * parity

    record_loads = []
    for chunk in range(chunks):
        at = pl.ds(chunk * rows, rows)
        record_loads.append(
            pltpu.make_async_copy(records_hbm.at[at, :], records.at[at, :], record_sem.at[chunk])
        )
    pairs = (
        (forward_hbm, forward), (channels_hbm, live_channels), (windows_hbm, live_windows),
        (inside_hbm, inside), (weight_hbm, weight), (inverse_hbm, inverse),
    )
    loads = [pltpu.make_async_copy(*pair, load_sem.at[n]) for n, pair in enumerate(pairs)]
    record_loads[0].start()
    for load in loads:
        load.start()
    for load in record_loads[1:]:
        load.start()

    barrier = pltpu.get_barrier_semaphore()
    for chan in (before, after, twin):
        pl.semaphore_signal(barrier, inc=1, device_id=(chan, hour), device_id_type=MESH)
    for step in range(1, n_hour):
        other = lax.rem(hour + step, n_hour)
        pl.semaphore_signal(barrier, inc=1, device_id=(me, other), device_id_type=MESH)

    def to_before(chunk):
        return pltpu.make_async_remote_copy(
            src_ref=own_send.at[chunk], dst_ref=far_two.at[chunk],
            send_sem=two_send.at[chunk], recv_sem=two_recv.at[chunk],
            device_id=(before, hour), device_id_type=MESH,
        )

    def to_twin(source, chunk):
        return pltpu.make_async_remote_copy(
            src_ref=source.at[chunk], dst_ref=far_one.at[chunk],
            send_sem=one_send.at[chunk], recv_sem=one_recv.at[chunk],
            device_id=(twin, hour), device_id_type=MESH,
        )

    def to_hour(step, distance):
        target = lax.rem(hour + distance, n_hour)
        return pltpu.make_async_remote_copy(
            src_ref=lagged.at[step, target], dst_ref=heard.at[step, distance - 1],
            send_sem=sum_send.at[step, distance - 1], recv_sem=sum_recv.at[step, distance - 1],
            device_id=(me, target), device_id_type=MESH,
        )

    for load in loads:
        load.wait()
    pl.semaphore_wait(barrier, 3 + n_hour - 1)

    def whiten_chunk(chunk, carry):
        start = pl.multiple_of(chunk * rows, rows)
        at = pl.ds(start, rows)
        pltpu.make_async_copy(
            records_hbm.at[at, :], records.at[at, :], record_sem.at[chunk]
        ).wait()
        spectra = jnp.dot(records[at, :], forward[...], preferred_element_type=jnp.float32)
        real_part = spectra[:, :BAND]
        imag_part = spectra[:, BAND:]
        amplitude = jnp.sqrt(real_part * real_part + imag_part * imag_part)
        high = amplitude.astype(jnp.bfloat16)
        low = (amplitude - high.astype(jnp.float32)).astype(jnp.bfloat16)
        smooth = jnp.dot(high, inside[...], preferred_element_type=jnp.float32)
        smooth = smooth + jnp.dot(low, inside[...], preferred_element_type=jnp.float32)
        row = lax.broadcasted_iota(jnp.int32, (rows, channels), 0)
        lane = lax.broadcasted_iota(jnp.int32, (rows, channels), 1)
        picked = jnp.where(lane == chunk * GROUP + row // windows, live_channels[...], 0)
        live = jnp.sum(picked.astype(jnp.float32), axis=1, keepdims=True)
        row = lax.broadcasted_iota(jnp.int32, (rows, windows), 0)
        lane = lax.broadcasted_iota(jnp.int32, (rows, windows), 1)
        picked = jnp.where(lane == row % windows, live_windows[...], 0)
        live = live * jnp.sum(picked.astype(jnp.float32), axis=1, keepdims=True)
        factor = live / (smooth * weight[...] + 1e-06)
        for tile in range(tiles):
            lanes = slice(tile * LANES, (tile + 1) * LANES)
            real = (real_part[:, lanes] * factor[:, lanes]).astype(jnp.bfloat16).astype(jnp.float32)
            imag = (imag_part[:, lanes] * factor[:, lanes]).astype(jnp.bfloat16).astype(jnp.float32)
            for kind, value in enumerate((real, imag, real - imag, real + imag)):
                own[kind, tile, at, :] = value
        for kind in range(2):
            for tile in range(tiles):
                for pair in range(windows // 2):
                    both = [
                        own[kind, tile, pl.ds(start + 2 * pair + part, GROUP, stride=windows), :]
                        for part in range(2)
                    ]
                    own_send[
                        chunk, pl.ds(pair * 2 * GROUP, 2 * GROUP),
                        pl.ds(kind * BAND + tile * LANES, LANES),
                    ] = jnp.concatenate(both, axis=0).astype(jnp.bfloat16)
        to_before(chunk).start()

        @pl.when(parity == 1)
        def _():
            to_twin(own_send, chunk).start()

        return carry

    lax.fori_loop(0, chunks, whiten_chunk, 0)

    def cross_lags(blocks):
        batch = 4
        count = len(blocks)
        for place, (source, chunk, _) in enumerate(blocks):
            for tile in range(tiles):
                real = source[chunk, :, pl.ds(tile * LANES, LANES)].astype(jnp.float32)
                imag = source[chunk, :, pl.ds(BAND + tile * LANES, LANES)].astype(jnp.float32)
                far[place, 0, tile] = real + imag
                far[place, 1, tile] = imag
                far[place, 2, tile] = real

        def tile_step(tile, carry):
            def channel_step(index, inner):
                sums = [[[None] * 3 for _ in range(batch)] for _ in range(count)]
                for window in range(windows):
                    at = pl.ds(window * GROUP, GROUP)
                    far_here = [[far[p, kind, tile, at, :] for kind in range(3)] for p in range(count)]
                    for part in range(batch):
                        base = pl.multiple_of((batch * index + part) * windows, windows)
                        for kind, stored in enumerate((0, 2, 3)):
                            mine = own[stored, tile, pl.ds(base + window, GROUP, stride=0), :]
                            for p in range(count):
                                term = mine * far_here[p][kind]
                                old = sums[p][part][kind]
                                sums[p][part][kind] = term if old is None else old + term
                size = batch * GROUP
                at = pl.ds(pl.multiple_of(index * size, size), size)
                lanes = pl.multiple_of(tile * LANES, LANES)
                for p in range(count):
                    reals = [k[0] - k[1] for k in sums[p]]
                    imags = [k[0] - k[2] for k in sums[p]]
                    cross[p, at, pl.ds(lanes, LANES)] = jnp.concatenate(reals, axis=0).astype(
                        jnp.bfloat16
                    )
                    cross[p, at, pl.ds(BAND + lanes, LANES)] = jnp.concatenate(
                        imags, axis=0
                    ).astype(jnp.bfloat16)
                return inner

            return lax.fori_loop(0, channels // batch, channel_step, carry)

        lax.fori_loop(0, tiles, tile_step, 0)
        for p, (_, _, step) in enumerate(blocks):
            result = jnp.dot(cross[p], inverse[...], preferred_element_type=jnp.float32)
            result = result * norm_factor
            for part in range(n_hour):
                lanes = slice(part * quarter, (part + 1) * quarter)
                lagged[step, part] = result[:, lanes].astype(jnp.bfloat16)
            for distance in range(1, n_hour):
                to_hour(step, distance).start()

    def finish(chunk, shift):
        step = 2 * chunk + shift
        value = lagged[step, hour].astype(jnp.float32)
        for distance in range(1, n_hour):
            to_hour(step, distance).wait()
            value = value + heard[step, distance - 1].astype(jnp.float32)
        at = pl.ds(pl.multiple_of(chunk * GROUP, GROUP), GROUP)
        total[:, shift, at, :] = value.reshape(channels, GROUP, quarter)

    def take_two(chunk):
        to_before(chunk).wait_recv()

        @pl.when(parity == 0)
        def _():
            to_twin(far_two, chunk).start()

    take_two(0)
    cross_lags([(far_two, 0, 1)])

    def correlate_chunk(chunk, carry):
        take_two(chunk + 1)
        to_twin(own_send, chunk).wait_recv()
        cross_lags([(far_two, chunk + 1, 2 * chunk + 3), (far_one, chunk, 2 * chunk)])

        @pl.when(chunk >= 1)
        def _():
            finish(chunk - 1, 1)

        @pl.when(chunk >= 2)
        def _():
            finish(chunk - 2, 0)

        return carry

    lax.fori_loop(0, chunks - 1, correlate_chunk, 0)
    last = chunks - 1
    to_twin(own_send, last).wait_recv()
    cross_lags([(far_one, last, 2 * last)])
    for chunk in range(chunks):
        to_before(chunk).wait_send()
        to_twin(own_send, chunk).wait_send()
    for chunk in range(max(chunks - 2, 0), chunks):
        finish(chunk, 1)
    for chunk in range(max(chunks - 3, 0), chunks):
        finish(chunk, 0)
    out[...] = total[...].astype(jnp.bfloat16)


def local(records, live_channels, live_windows):
    channels, windows, samples = records.shape
    n_chan, n_hour = lax.axis_size("chan"), lax.axis_size("hour")
    norm_factor = 1.0 / math.sqrt(windows * n_hour * BAND)
    chunks, rows, quarter = channels // GROUP, GROUP * windows, LAGS // n_hour
    steps = NSHIFT * chunks
    inside = band_inside()
    weight = (1.0 / inside.sum(axis=0, keepdims=True)).astype(np.float32)
    whitened = pltpu.VMEM((chunks, rows, 2 * BAND), jnp.bfloat16)
    return pl.pallas_call(
        functools.partial(kernel, n_chan, n_hour, channels, windows, norm_factor),
        out_shape=jax.ShapeDtypeStruct((channels, NSHIFT, channels, quarter), jnp.bfloat16),
        in_specs=[pl.BlockSpec(memory_space=pltpu.HBM)] * 7,
        out_specs=pl.BlockSpec(memory_space=pltpu.VMEM),
        scratch_shapes=[
            pltpu.VMEM((channels * windows, samples), jnp.bfloat16),
            pltpu.VMEM((1, channels), jnp.int32),
            pltpu.VMEM((1, windows), jnp.int32),
            pltpu.VMEM((SAMPLES, 2 * BAND), jnp.bfloat16),
            pltpu.VMEM((BAND, BAND), jnp.bfloat16),
            pltpu.VMEM((1, BAND), jnp.float32),
            pltpu.VMEM((2 * BAND, LAGS), jnp.bfloat16),
            pltpu.VMEM((4, BAND // LANES, channels * windows, LANES), jnp.float32),
            whitened,
            whitened,
            whitened,
            pltpu.VMEM((NSHIFT, 3, BAND // LANES, rows, LANES), jnp.float32),
            pltpu.VMEM((NSHIFT, channels * GROUP, 2 * BAND), jnp.bfloat16),
            pltpu.VMEM((steps, n_hour, channels * GROUP, quarter), jnp.bfloat16),
            pltpu.VMEM((steps, n_hour - 1, channels * GROUP, quarter), jnp.bfloat16),
            pltpu.VMEM((channels, NSHIFT, channels, quarter), jnp.float32),
            pltpu.SemaphoreType.DMA((6,)),
            pltpu.SemaphoreType.DMA((chunks,)),
            pltpu.SemaphoreType.DMA((chunks,)),
            pltpu.SemaphoreType.DMA((chunks,)),
            pltpu.SemaphoreType.DMA((chunks,)),
            pltpu.SemaphoreType.DMA((chunks,)),
            pltpu.SemaphoreType.DMA((steps, n_hour - 1)),
            pltpu.SemaphoreType.DMA((steps, n_hour - 1)),
        ],
        compiler_params=pltpu.CompilerParams(
            collective_id=0, has_side_effects=True, vmem_limit_bytes=64 * 1024 * 1024
        ),
        name="correlate",
    )(
        records.reshape(channels * windows, samples),
        live_channels.reshape(1, channels),
        live_windows.reshape(1, windows),
        jnp.asarray(forward_table()),
        jnp.asarray(inside.astype(ml_dtypes.bfloat16)),
        jnp.asarray(weight),
        jnp.asarray(inverse_table()),
    )


def solution(mesh):
    placed = (P("chan", "hour", None), P("chan"), P("hour"))
    return jax.shard_map(
        local, mesh=mesh, in_specs=placed, out_specs=P("chan", None, None, "hour"), check_vma=False
    )
```

```python
import functools
import math

import jax
import jax.numpy as jnp
import ml_dtypes
import numpy as np
from jax import lax
from jax.experimental import pallas as pl
from jax.experimental.pallas import tpu as pltpu
from jax.sharding import PartitionSpec as P

SAMPLES = 2048
BAND = 512
FIRST_BIN = 32
HALF = 64
LAGS = 512
NSHIFT = 2
GROUP = 8
LANES = 128
MESH = pl.DeviceIdType.MESH


def forward_table():
    times = np.arange(SAMPLES)[:, None]
    bins = FIRST_BIN + np.arange(BAND)[None, :]
    angle = (times * bins % SAMPLES) * (2.0 * math.pi / SAMPLES)
    return np.concatenate([np.cos(angle), -np.sin(angle)], axis=1).astype(ml_dtypes.bfloat16)


def inverse_table():
    bins = FIRST_BIN + np.arange(BAND)[:, None]
    shifts = np.arange(LAGS)[None, :] - LAGS // 2
    angle = (bins * shifts % SAMPLES) * (2.0 * math.pi / SAMPLES)
    return np.concatenate([np.cos(angle), -np.sin(angle)], axis=0).astype(ml_dtypes.bfloat16)


def band_inside():
    index = np.arange(BAND)
    return np.abs(index[:, None] - index[None, :]) <= HALF


def kernel(
    n_chan, n_hour, channels, windows, norm_factor,
    records_hbm, channels_hbm, windows_hbm, forward_hbm, inside_hbm, weight_hbm, inverse_hbm, total,
    records, live_channels, live_windows, forward, inside, weight, inverse,
    spectra, own, own_send, far_two, far_one, far, cross, lagged, heard,
    load_sem, record_sem, two_send, two_recv, one_send, one_recv, sum_send, sum_recv,
):
    chunks = channels // GROUP
    rows = GROUP * windows
    quarter = LAGS // n_hour
    tiles = BAND // LANES
    me = lax.axis_index("chan")
    hour = lax.axis_index("hour")
    parity = lax.rem(me, 2)
    before = lax.rem(me + n_chan - 2, n_chan)
    after = lax.rem(me + 2, n_chan)
    twin = me + 1 - 2 * parity

    record_loads = []
    for chunk in range(chunks):
        at = pl.ds(chunk * rows, rows)
        record_loads.append(
            pltpu.make_async_copy(records_hbm.at[at, :], records.at[at, :], record_sem.at[chunk])
        )
    pairs = (
        (forward_hbm, forward), (channels_hbm, live_channels), (windows_hbm, live_windows),
        (inside_hbm, inside), (weight_hbm, weight), (inverse_hbm, inverse),
    )
    loads = [pltpu.make_async_copy(*pair, load_sem.at[n]) for n, pair in enumerate(pairs)]
    record_loads[0].start()
    for load in loads:
        load.start()
    for load in record_loads[1:]:
        load.start()

    barrier = pltpu.get_barrier_semaphore()
    for chan in (before, after, twin):
        pl.semaphore_signal(barrier, inc=1, device_id=(chan, hour), device_id_type=MESH)
    for step in range(1, n_hour):
        other = lax.rem(hour + step, n_hour)
        pl.semaphore_signal(barrier, inc=1, device_id=(me, other), device_id_type=MESH)

    def to_before(chunk):
        return pltpu.make_async_remote_copy(
            src_ref=own_send.at[chunk], dst_ref=far_two.at[chunk],
            send_sem=two_send.at[chunk], recv_sem=two_recv.at[chunk],
            device_id=(before, hour), device_id_type=MESH,
        )

    def to_twin(source, chunk):
        return pltpu.make_async_remote_copy(
            src_ref=source.at[chunk], dst_ref=far_one.at[chunk],
            send_sem=one_send.at[chunk], recv_sem=one_recv.at[chunk],
            device_id=(twin, hour), device_id_type=MESH,
        )

    def to_hour(step, distance):
        target = lax.rem(hour + distance, n_hour)
        return pltpu.make_async_remote_copy(
            src_ref=lagged.at[step, target], dst_ref=heard.at[step, distance - 1],
            send_sem=sum_send.at[step, distance - 1], recv_sem=sum_recv.at[step, distance - 1],
            device_id=(me, target), device_id_type=MESH,
        )

    for load in loads:
        load.wait()
    pl.semaphore_wait(barrier, 3 + n_hour - 1)

    def whiten_chunk(chunk, carry):
        start = pl.multiple_of(chunk * rows, rows)
        at = pl.ds(start, rows)
        real_part = spectra[at, :BAND]
        imag_part = spectra[at, BAND:]
        amplitude = jnp.sqrt(real_part * real_part + imag_part * imag_part)
        high = amplitude.astype(jnp.bfloat16)
        low = (amplitude - high.astype(jnp.float32)).astype(jnp.bfloat16)
        smooth = jnp.dot(
            jnp.concatenate([high, low], axis=0), inside[...], preferred_element_type=jnp.float32
        )
        smooth = smooth[:rows] + smooth[rows:]
        row = lax.broadcasted_iota(jnp.int32, (rows, channels), 0)
        lane = lax.broadcasted_iota(jnp.int32, (rows, channels), 1)
        picked = jnp.where(lane == chunk * GROUP + row // windows, live_channels[...], 0)
        live = jnp.sum(picked.astype(jnp.float32), axis=1, keepdims=True)
        row = lax.broadcasted_iota(jnp.int32, (rows, windows), 0)
        lane = lax.broadcasted_iota(jnp.int32, (rows, windows), 1)
        picked = jnp.where(lane == row % windows, live_windows[...], 0)
        live = live * jnp.sum(picked.astype(jnp.float32), axis=1, keepdims=True)
        factor = live / (smooth * weight[...] + 1e-06)
        for tile in range(tiles):
            lanes = slice(tile * LANES, (tile + 1) * LANES)
            real = (real_part[:, lanes] * factor[:, lanes]).astype(jnp.bfloat16).astype(jnp.float32)
            imag = (imag_part[:, lanes] * factor[:, lanes]).astype(jnp.bfloat16).astype(jnp.float32)
            for kind, value in enumerate((real, imag, real - imag, real + imag)):
                own[kind, tile, at, :] = value
        for kind in range(2):
            for tile in range(tiles):
                for pair in range(windows // 2):
                    both = [
                        own[kind, tile, pl.ds(start + 2 * pair + part, GROUP, stride=windows), :]
                        for part in range(2)
                    ]
                    own_send[
                        chunk, pl.ds(pair * 2 * GROUP, 2 * GROUP),
                        pl.ds(kind * BAND + tile * LANES, LANES),
                    ] = jnp.concatenate(both, axis=0).astype(jnp.bfloat16)
        to_before(chunk).start()

        @pl.when(parity == 1)
        def _():
            to_twin(own_send, chunk).start()

        return carry

    def transform(first, count):
        at = pl.ds(first * rows, count * rows)
        for load in record_loads[first : first + count]:
            load.wait()
        spectra[at, :] = jnp.dot(records[at, :], forward[...], preferred_element_type=jnp.float32)

    transform(0, 1)
    whiten_chunk(0, 0)
    transform(1, chunks - 1)
    lax.fori_loop(1, chunks, whiten_chunk, 0)

    def cross_lags(blocks):
        count = len(blocks)
        batch = 8 // count
        for place, (source, chunk, _) in enumerate(blocks):
            for tile in range(tiles):
                real = source[chunk, :, pl.ds(tile * LANES, LANES)].astype(jnp.float32)
                imag = source[chunk, :, pl.ds(BAND + tile * LANES, LANES)].astype(jnp.float32)
                far[place, 0, tile] = real + imag
                far[place, 1, tile] = imag
                far[place, 2, tile] = real

        def tile_step(tile, carry):
            def channel_step(index, inner):
                sums = [[[None] * 3 for _ in range(batch)] for _ in range(count)]
                for window in range(windows):
                    at = pl.ds(window * GROUP, GROUP)
                    far_here = [[far[p, kind, tile, at, :] for kind in range(3)] for p in range(count)]
                    for part in range(batch):
                        base = pl.multiple_of((batch * index + part) * windows, windows)
                        for kind, stored in enumerate((0, 2, 3)):
                            mine = own[stored, tile, pl.ds(base + window, GROUP, stride=0), :]
                            for p in range(count):
                                term = mine * far_here[p][kind]
                                old = sums[p][part][kind]
                                sums[p][part][kind] = term if old is None else old + term
                size = batch * GROUP
                at = pl.ds(pl.multiple_of(index * size, size), size)
                lanes = pl.multiple_of(tile * LANES, LANES)
                for p in range(count):
                    reals = [k[0] - k[1] for k in sums[p]]
                    imags = [k[0] - k[2] for k in sums[p]]
                    cross[p, at, pl.ds(lanes, LANES)] = jnp.concatenate(reals, axis=0).astype(
                        jnp.bfloat16
                    )
                    cross[p, at, pl.ds(BAND + lanes, LANES)] = jnp.concatenate(
                        imags, axis=0
                    ).astype(jnp.bfloat16)
                return inner

            return lax.fori_loop(0, channels // batch, channel_step, carry)

        lax.fori_loop(0, tiles, tile_step, 0)
        for p, (_, _, step) in enumerate(blocks):
            result = jnp.dot(cross[p], inverse[...], preferred_element_type=jnp.float32)
            result = result * norm_factor
            for part in range(n_hour):
                lanes = slice(part * quarter, (part + 1) * quarter)
                lagged[step, part] = result[:, lanes].astype(jnp.bfloat16)
            for distance in range(1, n_hour):
                to_hour(step, distance).start()

    def finish(chunk, shift):
        step = 2 * chunk + shift
        value = lagged[step, hour].astype(jnp.float32)
        for distance in range(1, n_hour):
            to_hour(step, distance).wait()
            value = value + heard[step, distance - 1].astype(jnp.float32)
        at = pl.ds(pl.multiple_of(chunk * GROUP, GROUP), GROUP)
        total[:, shift, at, :] = value.reshape(channels, GROUP, quarter)

    def take_two(chunk):
        to_before(chunk).wait_recv()

        @pl.when(parity == 0)
        def _():
            to_twin(far_two, chunk).start()

    take_two(0)
    cross_lags([(far_two, 0, 1)])

    def correlate_chunk(chunk, carry):
        take_two(chunk + 1)
        to_twin(own_send, chunk).wait_recv()
        cross_lags([(far_two, chunk + 1, 2 * chunk + 3), (far_one, chunk, 2 * chunk)])

        @pl.when(chunk >= 1)
        def _():
            finish(chunk - 1, 1)

        @pl.when(chunk >= 2)
        def _():
            finish(chunk - 2, 0)

        return carry

    lax.fori_loop(0, chunks - 1, correlate_chunk, 0)
    last = chunks - 1
    to_twin(own_send, last).wait_recv()
    cross_lags([(far_one, last, 2 * last)])
    for chunk in range(chunks):
        to_before(chunk).wait_send()
        to_twin(own_send, chunk).wait_send()
    for chunk in range(max(chunks - 2, 0), chunks):
        finish(chunk, 1)
    for chunk in range(max(chunks - 3, 0), chunks):
        finish(chunk, 0)


def local(records, live_channels, live_windows):
    channels, windows, samples = records.shape
    n_chan, n_hour = lax.axis_size("chan"), lax.axis_size("hour")
    norm_factor = 1.0 / math.sqrt(windows * n_hour * BAND)
    chunks, rows, quarter = channels // GROUP, GROUP * windows, LAGS // n_hour
    steps = NSHIFT * chunks
    inside = band_inside()
    weight = (1.0 / inside.sum(axis=0, keepdims=True)).astype(np.float32)
    whitened = pltpu.VMEM((chunks, rows, 2 * BAND), jnp.bfloat16)
    return pl.pallas_call(
        functools.partial(kernel, n_chan, n_hour, channels, windows, norm_factor),
        out_shape=jax.ShapeDtypeStruct((channels, NSHIFT, channels, quarter), jnp.float32),
        in_specs=[pl.BlockSpec(memory_space=pltpu.HBM)] * 7,
        out_specs=pl.BlockSpec(memory_space=pltpu.VMEM),
        scratch_shapes=[
            pltpu.VMEM((channels * windows, samples), jnp.bfloat16),
            pltpu.VMEM((1, channels), jnp.int32),
            pltpu.VMEM((1, windows), jnp.int32),
            pltpu.VMEM((SAMPLES, 2 * BAND), jnp.bfloat16),
            pltpu.VMEM((BAND, BAND), jnp.bfloat16),
            pltpu.VMEM((1, BAND), jnp.float32),
            pltpu.VMEM((2 * BAND, LAGS), jnp.bfloat16),
            pltpu.VMEM((channels * windows, 2 * BAND), jnp.float32),
            pltpu.VMEM((4, BAND // LANES, channels * windows, LANES), jnp.float32),
            whitened,
            whitened,
            whitened,
            pltpu.VMEM((NSHIFT, 3, BAND // LANES, rows, LANES), jnp.float32),
            pltpu.VMEM((NSHIFT, channels * GROUP, 2 * BAND), jnp.bfloat16),
            pltpu.VMEM((steps, n_hour, channels * GROUP, quarter), jnp.bfloat16),
            pltpu.VMEM((steps, n_hour - 1, channels * GROUP, quarter), jnp.bfloat16),
            pltpu.SemaphoreType.DMA((6,)),
            pltpu.SemaphoreType.DMA((chunks,)),
            pltpu.SemaphoreType.DMA((chunks,)),
            pltpu.SemaphoreType.DMA((chunks,)),
            pltpu.SemaphoreType.DMA((chunks,)),
            pltpu.SemaphoreType.DMA((chunks,)),
            pltpu.SemaphoreType.DMA((steps, n_hour - 1)),
            pltpu.SemaphoreType.DMA((steps, n_hour - 1)),
        ],
        compiler_params=pltpu.CompilerParams(
            collective_id=0, has_side_effects=True, vmem_limit_bytes=64 * 1024 * 1024
        ),
        name="correlate",
    )(
        records.reshape(channels * windows, samples),
        live_channels.reshape(1, channels),
        live_windows.reshape(1, windows),
        jnp.asarray(forward_table()),
        jnp.asarray(inside.astype(ml_dtypes.bfloat16)),
        jnp.asarray(weight),
        jnp.asarray(inverse_table()),
    ).astype(jnp.bfloat16)


def solution(mesh):
    placed = (P("chan", "hour", None), P("chan"), P("hour"))
    return jax.shard_map(
        local, mesh=mesh, in_specs=placed, out_specs=P("chan", None, None, "hour"), check_vma=False
    )
```

```python
import functools
import math

import jax
import jax.numpy as jnp
import ml_dtypes
import numpy as np
from jax import lax
from jax.experimental import pallas as pl
from jax.experimental.pallas import tpu as pltpu
from jax.sharding import PartitionSpec as P

SAMPLES = 2048
BAND = 512
FIRST_BIN = 32
HALF = 64
LAGS = 512
NSHIFT = 2
GROUP = 8
LANES = 128
MESH = pl.DeviceIdType.MESH


def forward_table():
    times = np.arange(SAMPLES)[:, None]
    bins = FIRST_BIN + np.arange(BAND)[None, :]
    angle = (times * bins % SAMPLES) * (2.0 * math.pi / SAMPLES)
    return np.concatenate([np.cos(angle), -np.sin(angle)], axis=1).astype(ml_dtypes.bfloat16)


def inverse_table():
    bins = FIRST_BIN + np.arange(BAND)[:, None]
    shifts = np.arange(LAGS)[None, :] - LAGS // 2
    angle = (bins * shifts % SAMPLES) * (2.0 * math.pi / SAMPLES)
    return np.concatenate([np.cos(angle), -np.sin(angle)], axis=0).astype(ml_dtypes.bfloat16)


def band_inside():
    index = np.arange(BAND)
    return np.abs(index[:, None] - index[None, :]) <= HALF


def kernel(
    n_chan, n_hour, channels, windows, norm_factor,
    records_hbm, channels_hbm, windows_hbm, forward_hbm, inside_hbm, weight_hbm, inverse_hbm, out,
    records, live_channels, live_windows, forward, inside, weight, inverse,
    spectra, own, own_send, far_two, far_one, far, cross, lagged, near, joined, heard, total,
    load_sem, record_sem, two_send, two_recv, one_send, one_recv, near_send, near_recv, sum_send, sum_recv,
):
    chunks = channels // GROUP
    rows = GROUP * windows
    quarter = LAGS // n_hour
    tiles = BAND // LANES
    me = lax.axis_index("chan")
    hour = lax.axis_index("hour")
    parity = lax.rem(me, 2)
    before = lax.rem(me + n_chan - 2, n_chan)
    after = lax.rem(me + 2, n_chan)
    twin = me + 1 - 2 * parity
    core = lax.rem(hour, 2)
    chip = hour // 2
    other_core = hour + 1 - 2 * core
    other_chip = lax.rem(hour + 2, 4)

    record_loads = []
    for chunk in range(chunks):
        at = pl.ds(chunk * rows, rows)
        record_loads.append(
            pltpu.make_async_copy(records_hbm.at[at, :], records.at[at, :], record_sem.at[chunk])
        )
    pairs = (
        (forward_hbm, forward), (channels_hbm, live_channels), (windows_hbm, live_windows),
        (inside_hbm, inside), (weight_hbm, weight), (inverse_hbm, inverse),
    )
    loads = [pltpu.make_async_copy(*pair, load_sem.at[n]) for n, pair in enumerate(pairs)]
    record_loads[0].start()
    for load in loads:
        load.start()
    for load in record_loads[1:]:
        load.start()

    barrier = pltpu.get_barrier_semaphore()
    for chan in (before, after, twin):
        pl.semaphore_signal(barrier, inc=1, device_id=(chan, hour), device_id_type=MESH)
    for other in (other_core, other_chip):
        pl.semaphore_signal(barrier, inc=1, device_id=(me, other), device_id_type=MESH)

    def to_before(chunk):
        return pltpu.make_async_remote_copy(
            src_ref=own_send.at[chunk], dst_ref=far_two.at[chunk],
            send_sem=two_send.at[chunk], recv_sem=two_recv.at[chunk],
            device_id=(before, hour), device_id_type=MESH,
        )

    def to_twin(source, chunk):
        return pltpu.make_async_remote_copy(
            src_ref=source.at[chunk], dst_ref=far_one.at[chunk],
            send_sem=one_send.at[chunk], recv_sem=one_recv.at[chunk],
            device_id=(twin, hour), device_id_type=MESH,
        )

    def to_core(step):
        return pltpu.make_async_remote_copy(
            src_ref=lagged.at[step, 1 - core], dst_ref=near.at[step],
            send_sem=near_send.at[step], recv_sem=near_recv.at[step],
            device_id=(me, other_core), device_id_type=MESH,
        )

    def to_chip(step):
        return pltpu.make_async_remote_copy(
            src_ref=joined.at[step], dst_ref=heard.at[step],
            send_sem=sum_send.at[step], recv_sem=sum_recv.at[step],
            device_id=(me, other_chip), device_id_type=MESH,
        )

    for load in loads:
        load.wait()
    pl.semaphore_wait(barrier, 5)

    def whiten_chunk(chunk, carry):
        start = pl.multiple_of(chunk * rows, rows)
        at = pl.ds(start, rows)
        real_part = spectra[at, :BAND]
        imag_part = spectra[at, BAND:]
        amplitude = jnp.sqrt(real_part * real_part + imag_part * imag_part)
        high = amplitude.astype(jnp.bfloat16)
        low = (amplitude - high.astype(jnp.float32)).astype(jnp.bfloat16)
        smooth = jnp.dot(
            jnp.concatenate([high, low], axis=0), inside[...], preferred_element_type=jnp.float32
        )
        smooth = smooth[:rows] + smooth[rows:]
        row = lax.broadcasted_iota(jnp.int32, (rows, channels), 0)
        lane = lax.broadcasted_iota(jnp.int32, (rows, channels), 1)
        picked = jnp.where(lane == chunk * GROUP + row // windows, live_channels[...], 0)
        live = jnp.sum(picked.astype(jnp.float32), axis=1, keepdims=True)
        row = lax.broadcasted_iota(jnp.int32, (rows, windows), 0)
        lane = lax.broadcasted_iota(jnp.int32, (rows, windows), 1)
        picked = jnp.where(lane == row % windows, live_windows[...], 0)
        live = live * jnp.sum(picked.astype(jnp.float32), axis=1, keepdims=True)
        factor = live / (smooth * weight[...] + 1e-06)
        for tile in range(tiles):
            lanes = slice(tile * LANES, (tile + 1) * LANES)
            real = (real_part[:, lanes] * factor[:, lanes]).astype(jnp.bfloat16).astype(jnp.float32)
            imag = (imag_part[:, lanes] * factor[:, lanes]).astype(jnp.bfloat16).astype(jnp.float32)
            for kind, value in enumerate((real, imag, real - imag, real + imag)):
                own[kind, tile, at, :] = value
        for kind in range(2):
            for tile in range(tiles):
                for pair in range(windows // 2):
                    both = [
                        own[kind, tile, pl.ds(start + 2 * pair + part, GROUP, stride=windows), :]
                        for part in range(2)
                    ]
                    own_send[
                        chunk, pl.ds(pair * 2 * GROUP, 2 * GROUP),
                        pl.ds(kind * BAND + tile * LANES, LANES),
                    ] = jnp.concatenate(both, axis=0).astype(jnp.bfloat16)
        to_before(chunk).start()

        @pl.when(parity == 1)
        def _():
            to_twin(own_send, chunk).start()

        return carry

    def transform(first, count):
        at = pl.ds(first * rows, count * rows)
        for load in record_loads[first : first + count]:
            load.wait()
        spectra[at, :] = jnp.dot(records[at, :], forward[...], preferred_element_type=jnp.float32)

    transform(0, 1)
    whiten_chunk(0, 0)
    transform(1, chunks - 1)
    lax.fori_loop(1, chunks, whiten_chunk, 0)

    def cross_lags(blocks, between):
        count = len(blocks)
        batch = 8 // count
        for place, (source, chunk, _) in enumerate(blocks):
            for tile in range(tiles):
                real = source[chunk, :, pl.ds(tile * LANES, LANES)].astype(jnp.float32)
                imag = source[chunk, :, pl.ds(BAND + tile * LANES, LANES)].astype(jnp.float32)
                far[place, 0, tile] = real + imag
                far[place, 1, tile] = imag
                far[place, 2, tile] = real

        def tile_step(tile, carry):
            def channel_step(index, inner):
                sums = [[[None] * 3 for _ in range(batch)] for _ in range(count)]
                for window in range(windows):
                    at = pl.ds(window * GROUP, GROUP)
                    far_here = [[far[p, kind, tile, at, :] for kind in range(3)] for p in range(count)]
                    for part in range(batch):
                        base = pl.multiple_of((batch * index + part) * windows, windows)
                        for kind, stored in enumerate((0, 2, 3)):
                            mine = own[stored, tile, pl.ds(base + window, GROUP, stride=0), :]
                            for p in range(count):
                                term = mine * far_here[p][kind]
                                old = sums[p][part][kind]
                                sums[p][part][kind] = term if old is None else old + term
                size = batch * GROUP
                at = pl.ds(pl.multiple_of(index * size, size), size)
                lanes = pl.multiple_of(tile * LANES, LANES)
                for p in range(count):
                    reals = [k[0] - k[1] for k in sums[p]]
                    imags = [k[0] - k[2] for k in sums[p]]
                    cross[p, at, pl.ds(lanes, LANES)] = jnp.concatenate(reals, axis=0).astype(
                        jnp.bfloat16
                    )
                    cross[p, at, pl.ds(BAND + lanes, LANES)] = jnp.concatenate(
                        imags, axis=0
                    ).astype(jnp.bfloat16)
                return inner

            pl.when(tile == 1)(between)
            return lax.fori_loop(0, channels // batch, channel_step, carry)

        lax.fori_loop(0, tiles, tile_step, 0)
        for p, (_, _, step) in enumerate(blocks):
            result = jnp.dot(cross[p], inverse[...], preferred_element_type=jnp.float32)
            result = result * norm_factor
            for part in range(n_hour):
                lanes = slice(part * quarter, (part + 1) * quarter)
                lagged[step, part % 2, part // 2] = result[:, lanes].astype(jnp.bfloat16)
            to_core(step).start()

    def relay(step):
        to_core(step).wait_recv()
        mine = lagged[step, core, 1 - chip].astype(jnp.float32)
        mine = mine + near[step, 1 - chip].astype(jnp.float32)
        joined[step] = mine.astype(jnp.bfloat16)
        to_chip(step).start()

    def finish(chunk, shift):
        step = 2 * chunk + shift
        to_core(step).wait_send()
        to_chip(step).wait()
        value = lagged[step, core, chip].astype(jnp.float32)
        value = value + near[step, chip].astype(jnp.float32) + heard[step].astype(jnp.float32)
        at = pl.ds(pl.multiple_of(chunk * GROUP, GROUP), GROUP)
        total[:, shift, at, :] = value.reshape(channels, GROUP, quarter)

    def take_two(chunk):
        to_before(chunk).wait_recv()

        @pl.when(parity == 0)
        def _():
            to_twin(far_two, chunk).start()

    take_two(0)
    cross_lags([(far_two, 0, 1)], lambda: None)

    def correlate_chunk(chunk, carry):
        take_two(chunk + 1)
        to_twin(own_send, chunk).wait_recv()
        def between():
            relay(2 * chunk + 1)

            @pl.when(chunk >= 1)
            def _():
                relay(2 * chunk - 2)

        cross_lags([(far_two, chunk + 1, 2 * chunk + 3), (far_one, chunk, 2 * chunk)], between)

        @pl.when(chunk >= 1)
        def _():
            finish(chunk - 1, 1)

        @pl.when(chunk >= 2)
        def _():
            finish(chunk - 2, 0)

        return carry

    lax.fori_loop(0, chunks - 1, correlate_chunk, 0)
    last = chunks - 1
    to_twin(own_send, last).wait_recv()

    def between_last():
        relay(2 * last + 1)
        relay(2 * last - 2)

    cross_lags([(far_one, last, 2 * last)], between_last)
    relay(2 * last)
    for chunk in range(chunks):
        to_before(chunk).wait_send()
        to_twin(own_send, chunk).wait_send()
    for chunk in range(max(chunks - 2, 0), chunks):
        finish(chunk, 1)
    for chunk in range(max(chunks - 3, 0), chunks):
        finish(chunk, 0)
    out[...] = total[...].astype(jnp.bfloat16)


def local(records, live_channels, live_windows):
    channels, windows, samples = records.shape
    n_chan, n_hour = lax.axis_size("chan"), lax.axis_size("hour")
    norm_factor = 1.0 / math.sqrt(windows * n_hour * BAND)
    chunks, rows, quarter = channels // GROUP, GROUP * windows, LAGS // n_hour
    steps = NSHIFT * chunks
    inside = band_inside()
    weight = (1.0 / inside.sum(axis=0, keepdims=True)).astype(np.float32)
    whitened = pltpu.VMEM((chunks, rows, 2 * BAND), jnp.bfloat16)
    return pl.pallas_call(
        functools.partial(kernel, n_chan, n_hour, channels, windows, norm_factor),
        out_shape=jax.ShapeDtypeStruct((channels, NSHIFT, channels, quarter), jnp.bfloat16),
        in_specs=[pl.BlockSpec(memory_space=pltpu.HBM)] * 7,
        out_specs=pl.BlockSpec(memory_space=pltpu.VMEM),
        scratch_shapes=[
            pltpu.VMEM((channels * windows, samples), jnp.bfloat16),
            pltpu.VMEM((1, channels), jnp.int32),
            pltpu.VMEM((1, windows), jnp.int32),
            pltpu.VMEM((SAMPLES, 2 * BAND), jnp.bfloat16),
            pltpu.VMEM((BAND, BAND), jnp.bfloat16),
            pltpu.VMEM((1, BAND), jnp.float32),
            pltpu.VMEM((2 * BAND, LAGS), jnp.bfloat16),
            pltpu.VMEM((channels * windows, 2 * BAND), jnp.float32),
            pltpu.VMEM((4, BAND // LANES, channels * windows, LANES), jnp.float32),
            whitened,
            whitened,
            whitened,
            pltpu.VMEM((NSHIFT, 3, BAND // LANES, rows, LANES), jnp.float32),
            pltpu.VMEM((NSHIFT, channels * GROUP, 2 * BAND), jnp.bfloat16),
            pltpu.VMEM((steps, 2, n_hour // 2, channels * GROUP, quarter), jnp.bfloat16),
            pltpu.VMEM((steps, n_hour // 2, channels * GROUP, quarter), jnp.bfloat16),
            pltpu.VMEM((steps, channels * GROUP, quarter), jnp.bfloat16),
            pltpu.VMEM((steps, channels * GROUP, quarter), jnp.bfloat16),
            pltpu.VMEM((channels, NSHIFT, channels, quarter), jnp.float32),
            pltpu.SemaphoreType.DMA((6,)),
            pltpu.SemaphoreType.DMA((chunks,)),
            pltpu.SemaphoreType.DMA((chunks,)),
            pltpu.SemaphoreType.DMA((chunks,)),
            pltpu.SemaphoreType.DMA((chunks,)),
            pltpu.SemaphoreType.DMA((chunks,)),
            pltpu.SemaphoreType.DMA((steps,)),
            pltpu.SemaphoreType.DMA((steps,)),
            pltpu.SemaphoreType.DMA((steps,)),
            pltpu.SemaphoreType.DMA((steps,)),
        ],
        compiler_params=pltpu.CompilerParams(
            collective_id=0, has_side_effects=True, vmem_limit_bytes=64 * 1024 * 1024
        ),
        name="correlate",
    )(
        records.reshape(channels * windows, samples),
        live_channels.reshape(1, channels),
        live_windows.reshape(1, windows),
        jnp.asarray(forward_table()),
        jnp.asarray(inside.astype(ml_dtypes.bfloat16)),
        jnp.asarray(weight),
        jnp.asarray(inverse_table()),
    )


def solution(mesh):
    placed = (P("chan", "hour", None), P("chan"), P("hour"))
    return jax.shard_map(
        local, mesh=mesh, in_specs=placed, out_specs=P("chan", None, None, "hour"), check_vma=False
    )
```

```python
import functools
import math

import jax
import jax.numpy as jnp
import ml_dtypes
import numpy as np
from jax import lax
from jax.experimental import pallas as pl
from jax.experimental.pallas import tpu as pltpu
from jax.sharding import PartitionSpec as P

SAMPLES = 2048
BAND = 512
FIRST_BIN = 32
HALF = 64
LAGS = 512
NSHIFT = 2
GROUP = 8
LANES = 128
MESH = pl.DeviceIdType.MESH


def forward_table():
    times = np.arange(SAMPLES)[:, None]
    bins = FIRST_BIN + np.arange(BAND)[None, :]
    angle = (times * bins % SAMPLES) * (2.0 * math.pi / SAMPLES)
    return np.concatenate([np.cos(angle), -np.sin(angle)], axis=1).astype(ml_dtypes.bfloat16)


def inverse_table():
    bins = FIRST_BIN + np.arange(BAND)[:, None]
    shifts = np.arange(LAGS)[None, :] - LAGS // 2
    angle = (bins * shifts % SAMPLES) * (2.0 * math.pi / SAMPLES)
    return np.concatenate([np.cos(angle), -np.sin(angle)], axis=0).astype(ml_dtypes.bfloat16)


def band_inside():
    index = np.arange(BAND)
    return np.abs(index[:, None] - index[None, :]) <= HALF


def kernel(
    n_chan, n_hour, channels, windows, norm_factor,
    records_hbm, channels_hbm, windows_hbm, forward_hbm, inside_hbm, weight_hbm, inverse_hbm, out,
    records, live_channels, live_windows, forward, inside, weight, inverse,
    spectra, own, own_send, far_two, far_one, far, cross, lagged, near, joined, heard, total,
    load_sem, record_sem, two_send, two_recv, one_send, one_recv, near_send, near_recv, sum_send, sum_recv,
):
    chunks = channels // GROUP
    rows = GROUP * windows
    quarter = LAGS // n_hour
    tiles = BAND // LANES
    me = lax.axis_index("chan")
    hour = lax.axis_index("hour")
    parity = lax.rem(me, 2)
    before = lax.rem(me + n_chan - 2, n_chan)
    after = lax.rem(me + 2, n_chan)
    twin = me + 1 - 2 * parity
    core = lax.rem(hour, 2)
    chip = hour // 2
    other_core = hour + 1 - 2 * core
    other_chip = lax.rem(hour + 2, 4)

    record_loads = []
    for chunk in range(chunks):
        at = pl.ds(chunk * rows, rows)
        record_loads.append(
            pltpu.make_async_copy(records_hbm.at[at, :], records.at[at, :], record_sem.at[chunk])
        )
    pairs = (
        (forward_hbm, forward), (channels_hbm, live_channels), (windows_hbm, live_windows),
        (inside_hbm, inside), (weight_hbm, weight), (inverse_hbm, inverse),
    )
    loads = [pltpu.make_async_copy(*pair, load_sem.at[n]) for n, pair in enumerate(pairs)]
    record_loads[0].start()
    for load in loads:
        load.start()
    for load in record_loads[1:]:
        load.start()

    barrier = pltpu.get_barrier_semaphore()
    for chan in (before, after, twin):
        pl.semaphore_signal(barrier, inc=1, device_id=(chan, hour), device_id_type=MESH)
    for other in (other_core, other_chip):
        pl.semaphore_signal(barrier, inc=1, device_id=(me, other), device_id_type=MESH)

    def to_before(chunk, tile):
        return pltpu.make_async_remote_copy(
            src_ref=own_send.at[chunk, tile], dst_ref=far_two.at[chunk, tile],
            send_sem=two_send.at[chunk, tile], recv_sem=two_recv.at[chunk, tile],
            device_id=(before, hour), device_id_type=MESH,
        )

    def to_twin(source, chunk, tile):
        return pltpu.make_async_remote_copy(
            src_ref=source.at[chunk, tile], dst_ref=far_one.at[chunk, tile],
            send_sem=one_send.at[chunk, tile], recv_sem=one_recv.at[chunk, tile],
            device_id=(twin, hour), device_id_type=MESH,
        )

    def to_core(step):
        return pltpu.make_async_remote_copy(
            src_ref=lagged.at[step, 1 - core], dst_ref=near.at[step],
            send_sem=near_send.at[step], recv_sem=near_recv.at[step],
            device_id=(me, other_core), device_id_type=MESH,
        )

    def to_chip(step):
        return pltpu.make_async_remote_copy(
            src_ref=joined.at[step], dst_ref=heard.at[step],
            send_sem=sum_send.at[step], recv_sem=sum_recv.at[step],
            device_id=(me, other_chip), device_id_type=MESH,
        )

    for load in loads:
        load.wait()
    pl.semaphore_wait(barrier, 5)

    def whiten_chunk(chunk, carry):
        start = pl.multiple_of(chunk * rows, rows)
        at = pl.ds(start, rows)
        real_part = spectra[at, :BAND]
        imag_part = spectra[at, BAND:]
        amplitude = jnp.sqrt(real_part * real_part + imag_part * imag_part)
        high = amplitude.astype(jnp.bfloat16)
        low = (amplitude - high.astype(jnp.float32)).astype(jnp.bfloat16)
        smooth = jnp.dot(
            jnp.concatenate([high, low], axis=0), inside[...], preferred_element_type=jnp.float32
        )
        smooth = smooth[:rows] + smooth[rows:]
        row = lax.broadcasted_iota(jnp.int32, (rows, channels), 0)
        lane = lax.broadcasted_iota(jnp.int32, (rows, channels), 1)
        picked = jnp.where(lane == chunk * GROUP + row // windows, live_channels[...], 0)
        live = jnp.sum(picked.astype(jnp.float32), axis=1, keepdims=True)
        row = lax.broadcasted_iota(jnp.int32, (rows, windows), 0)
        lane = lax.broadcasted_iota(jnp.int32, (rows, windows), 1)
        picked = jnp.where(lane == row % windows, live_windows[...], 0)
        live = live * jnp.sum(picked.astype(jnp.float32), axis=1, keepdims=True)
        factor = live / (smooth * weight[...] + 1e-06)
        for tile in range(tiles):
            lanes = slice(tile * LANES, (tile + 1) * LANES)
            real = (real_part[:, lanes] * factor[:, lanes]).astype(jnp.bfloat16).astype(jnp.float32)
            imag = (imag_part[:, lanes] * factor[:, lanes]).astype(jnp.bfloat16).astype(jnp.float32)
            for kind, value in enumerate((real, imag, real - imag, real + imag)):
                own[kind, tile, at, :] = value
        for tile in range(tiles):
            for kind in range(2):
                for pair in range(windows // 2):
                    both = [
                        own[kind, tile, pl.ds(start + 2 * pair + part, GROUP, stride=windows), :]
                        for part in range(2)
                    ]
                    own_send[
                        chunk, tile, pl.ds(pair * 2 * GROUP, 2 * GROUP), pl.ds(kind * LANES, LANES)
                    ] = jnp.concatenate(both, axis=0).astype(jnp.bfloat16)
            to_before(chunk, tile).start()

            @pl.when(parity == 1)
            def _():
                to_twin(own_send, chunk, tile).start()

        return carry

    def transform(first, count):
        at = pl.ds(first * rows, count * rows)
        for load in record_loads[first : first + count]:
            load.wait()
        spectra[at, :] = jnp.dot(records[at, :], forward[...], preferred_element_type=jnp.float32)

    transform(0, 1)
    whiten_chunk(0, 0)
    transform(1, chunks - 1)
    lax.fori_loop(1, chunks, whiten_chunk, 0)

    def cross_lags(blocks, between):
        count = len(blocks)
        batch = 8 // count
        def tile_step(tile, carry):
            for place, (source, chunk, _) in enumerate(blocks):
                if source is far_two:
                    to_before(chunk, tile).wait_recv()

                    @pl.when(parity == 0)
                    def _():
                        to_twin(far_two, chunk, tile).start()

                else:
                    to_twin(own_send, chunk, tile).wait_recv()
            for place, (source, chunk, _) in enumerate(blocks):
                real = source[chunk, tile, :, :LANES].astype(jnp.float32)
                imag = source[chunk, tile, :, LANES:].astype(jnp.float32)
                far[place, 0] = real + imag
                far[place, 1] = imag
                far[place, 2] = real

            def channel_step(index, inner):
                sums = [[[None] * 3 for _ in range(batch)] for _ in range(count)]
                for window in range(windows):
                    at = pl.ds(window * GROUP, GROUP)
                    far_here = [[far[p, kind, at, :] for kind in range(3)] for p in range(count)]
                    for part in range(batch):
                        base = pl.multiple_of((batch * index + part) * windows, windows)
                        for kind, stored in enumerate((0, 2, 3)):
                            mine = own[stored, tile, pl.ds(base + window, GROUP, stride=0), :]
                            for p in range(count):
                                term = mine * far_here[p][kind]
                                old = sums[p][part][kind]
                                sums[p][part][kind] = term if old is None else old + term
                size = batch * GROUP
                at = pl.ds(pl.multiple_of(index * size, size), size)
                lanes = pl.multiple_of(tile * LANES, LANES)
                for p in range(count):
                    reals = [k[0] - k[1] for k in sums[p]]
                    imags = [k[0] - k[2] for k in sums[p]]
                    cross[p, at, pl.ds(lanes, LANES)] = jnp.concatenate(reals, axis=0).astype(
                        jnp.bfloat16
                    )
                    cross[p, at, pl.ds(BAND + lanes, LANES)] = jnp.concatenate(
                        imags, axis=0
                    ).astype(jnp.bfloat16)
                return inner

            pl.when(tile == 1)(between)
            return lax.fori_loop(0, channels // batch, channel_step, carry)

        lax.fori_loop(0, tiles, tile_step, 0)
        for p, (_, _, step) in enumerate(blocks):
            result = jnp.dot(cross[p], inverse[...], preferred_element_type=jnp.float32)
            result = result * norm_factor
            for part in range(n_hour):
                lanes = slice(part * quarter, (part + 1) * quarter)
                lagged[step, part % 2, part // 2] = result[:, lanes].astype(jnp.bfloat16)
            to_core(step).start()

    def relay(step):
        to_core(step).wait_recv()
        mine = lagged[step, core, 1 - chip].astype(jnp.float32)
        mine = mine + near[step, 1 - chip].astype(jnp.float32)
        joined[step] = mine.astype(jnp.bfloat16)
        to_chip(step).start()

    def finish(chunk, shift):
        step = 2 * chunk + shift
        to_core(step).wait_send()
        to_chip(step).wait()
        value = lagged[step, core, chip].astype(jnp.float32)
        value = value + near[step, chip].astype(jnp.float32) + heard[step].astype(jnp.float32)
        at = pl.ds(pl.multiple_of(chunk * GROUP, GROUP), GROUP)
        total[:, shift, at, :] = value.reshape(channels, GROUP, quarter)

    cross_lags([(far_two, 0, 1)], lambda: None)

    def correlate_chunk(chunk, carry):
        def between():
            relay(2 * chunk + 1)

            @pl.when(chunk >= 1)
            def _():
                relay(2 * chunk - 2)

        cross_lags([(far_two, chunk + 1, 2 * chunk + 3), (far_one, chunk, 2 * chunk)], between)

        @pl.when(chunk >= 1)
        def _():
            finish(chunk - 1, 1)

        @pl.when(chunk >= 2)
        def _():
            finish(chunk - 2, 0)

        return carry

    lax.fori_loop(0, chunks - 1, correlate_chunk, 0)
    last = chunks - 1

    def between_last():
        relay(2 * last + 1)
        relay(2 * last - 2)

    cross_lags([(far_one, last, 2 * last)], between_last)
    relay(2 * last)
    for chunk in range(chunks):
        for tile in range(tiles):
            to_before(chunk, tile).wait_send()
            to_twin(own_send, chunk, tile).wait_send()
    for chunk in range(max(chunks - 2, 0), chunks):
        finish(chunk, 1)
    for chunk in range(max(chunks - 3, 0), chunks):
        finish(chunk, 0)
    out[...] = total[...].astype(jnp.bfloat16)


def local(records, live_channels, live_windows):
    channels, windows, samples = records.shape
    n_chan, n_hour = lax.axis_size("chan"), lax.axis_size("hour")
    norm_factor = 1.0 / math.sqrt(windows * n_hour * BAND)
    chunks, rows, quarter = channels // GROUP, GROUP * windows, LAGS // n_hour
    steps = NSHIFT * chunks
    inside = band_inside()
    weight = (1.0 / inside.sum(axis=0, keepdims=True)).astype(np.float32)
    tiles = BAND // LANES
    whitened = pltpu.VMEM((chunks, tiles, rows, 2 * LANES), jnp.bfloat16)
    return pl.pallas_call(
        functools.partial(kernel, n_chan, n_hour, channels, windows, norm_factor),
        out_shape=jax.ShapeDtypeStruct((channels, NSHIFT, channels, quarter), jnp.bfloat16),
        in_specs=[pl.BlockSpec(memory_space=pltpu.HBM)] * 7,
        out_specs=pl.BlockSpec(memory_space=pltpu.VMEM),
        scratch_shapes=[
            pltpu.VMEM((channels * windows, samples), jnp.bfloat16),
            pltpu.VMEM((1, channels), jnp.int32),
            pltpu.VMEM((1, windows), jnp.int32),
            pltpu.VMEM((SAMPLES, 2 * BAND), jnp.bfloat16),
            pltpu.VMEM((BAND, BAND), jnp.bfloat16),
            pltpu.VMEM((1, BAND), jnp.float32),
            pltpu.VMEM((2 * BAND, LAGS), jnp.bfloat16),
            pltpu.VMEM((channels * windows, 2 * BAND), jnp.float32),
            pltpu.VMEM((4, BAND // LANES, channels * windows, LANES), jnp.float32),
            whitened,
            whitened,
            whitened,
            pltpu.VMEM((NSHIFT, 3, rows, LANES), jnp.float32),
            pltpu.VMEM((NSHIFT, channels * GROUP, 2 * BAND), jnp.bfloat16),
            pltpu.VMEM((steps, 2, n_hour // 2, channels * GROUP, quarter), jnp.bfloat16),
            pltpu.VMEM((steps, n_hour // 2, channels * GROUP, quarter), jnp.bfloat16),
            pltpu.VMEM((steps, channels * GROUP, quarter), jnp.bfloat16),
            pltpu.VMEM((steps, channels * GROUP, quarter), jnp.bfloat16),
            pltpu.VMEM((channels, NSHIFT, channels, quarter), jnp.float32),
            pltpu.SemaphoreType.DMA((6,)),
            pltpu.SemaphoreType.DMA((chunks,)),
            pltpu.SemaphoreType.DMA((chunks, tiles)),
            pltpu.SemaphoreType.DMA((chunks, tiles)),
            pltpu.SemaphoreType.DMA((chunks, tiles)),
            pltpu.SemaphoreType.DMA((chunks, tiles)),
            pltpu.SemaphoreType.DMA((steps,)),
            pltpu.SemaphoreType.DMA((steps,)),
            pltpu.SemaphoreType.DMA((steps,)),
            pltpu.SemaphoreType.DMA((steps,)),
        ],
        compiler_params=pltpu.CompilerParams(
            collective_id=0, has_side_effects=True, vmem_limit_bytes=64 * 1024 * 1024
        ),
        name="correlate",
    )(
        records.reshape(channels * windows, samples),
        live_channels.reshape(1, channels),
        live_windows.reshape(1, windows),
        jnp.asarray(forward_table()),
        jnp.asarray(inside.astype(ml_dtypes.bfloat16)),
        jnp.asarray(weight),
        jnp.asarray(inverse_table()),
    )


def solution(mesh):
    placed = (P("chan", "hour", None), P("chan"), P("hour"))
    return jax.shard_map(
        local, mesh=mesh, in_specs=placed, out_specs=P("chan", None, None, "hour"), check_vma=False
    )
```

```python
import functools
import math

import jax
import jax.numpy as jnp
import ml_dtypes
import numpy as np
from jax import lax
from jax.experimental import pallas as pl
from jax.experimental.pallas import tpu as pltpu
from jax.sharding import PartitionSpec as P

SAMPLES = 2048
BAND = 512
FIRST_BIN = 32
HALF = 64
LAGS = 512
NSHIFT = 2
GROUP = 8
LANES = 128
MESH = pl.DeviceIdType.MESH


def forward_table():
    times = np.arange(SAMPLES)[:, None]
    bins = FIRST_BIN + np.arange(BAND)[None, :]
    angle = (times * bins % SAMPLES) * (2.0 * math.pi / SAMPLES)
    return np.concatenate([np.cos(angle), -np.sin(angle)], axis=1).astype(ml_dtypes.bfloat16)


def inverse_table():
    bins = FIRST_BIN + np.arange(BAND)[:, None]
    shifts = np.arange(LAGS)[None, :] - LAGS // 2
    angle = (bins * shifts % SAMPLES) * (2.0 * math.pi / SAMPLES)
    return np.concatenate([np.cos(angle), -np.sin(angle)], axis=0).astype(ml_dtypes.bfloat16)


def band_inside():
    index = np.arange(BAND)
    return np.abs(index[:, None] - index[None, :]) <= HALF


def kernel(
    n_chan, n_hour, channels, windows, norm_factor,
    records_hbm, channels_hbm, windows_hbm, forward_hbm, inside_hbm, weight_hbm, inverse_hbm, out,
    records, live_channels, live_windows, forward, inside, weight, inverse,
    spectra, own, own_send, far_two, far_one, far, cross, lagged, near, joined, heard, total,
    load_sem, record_sem, two_send, two_recv, one_send, one_recv, near_send, near_recv, sum_send, sum_recv,
):
    chunks = channels // GROUP
    rows = GROUP * windows
    quarter = LAGS // n_hour
    tiles = BAND // LANES
    me = lax.axis_index("chan")
    hour = lax.axis_index("hour")
    parity = lax.rem(me, 2)
    before = lax.rem(me + n_chan - 2, n_chan)
    after = lax.rem(me + 2, n_chan)
    twin = me + 1 - 2 * parity
    core = lax.rem(hour, 2)
    chip = hour // 2
    other_core = hour + 1 - 2 * core
    other_chip = lax.rem(hour + 2, 4)

    record_loads = []
    for chunk in range(chunks):
        at = pl.ds(chunk * rows, rows)
        record_loads.append(
            pltpu.make_async_copy(records_hbm.at[at, :], records.at[at, :], record_sem.at[chunk])
        )
    pairs = (
        (forward_hbm, forward), (channels_hbm, live_channels), (windows_hbm, live_windows),
        (inside_hbm, inside), (weight_hbm, weight), (inverse_hbm, inverse),
    )
    loads = [pltpu.make_async_copy(*pair, load_sem.at[n]) for n, pair in enumerate(pairs)]
    record_loads[0].start()
    for load in loads[:-1]:
        load.start()

    barrier = pltpu.get_barrier_semaphore()
    for chan in (before, after, twin):
        pl.semaphore_signal(barrier, inc=1, device_id=(chan, hour), device_id_type=MESH)
    for other in (other_core, other_chip):
        pl.semaphore_signal(barrier, inc=1, device_id=(me, other), device_id_type=MESH)

    def to_before(chunk, tile):
        return pltpu.make_async_remote_copy(
            src_ref=own_send.at[chunk, tile], dst_ref=far_two.at[chunk, tile],
            send_sem=two_send.at[chunk, tile], recv_sem=two_recv.at[chunk, tile],
            device_id=(before, hour), device_id_type=MESH,
        )

    def to_twin(source, chunk, tile):
        return pltpu.make_async_remote_copy(
            src_ref=source.at[chunk, tile], dst_ref=far_one.at[chunk, tile],
            send_sem=one_send.at[chunk, tile], recv_sem=one_recv.at[chunk, tile],
            device_id=(twin, hour), device_id_type=MESH,
        )

    def to_core(step):
        return pltpu.make_async_remote_copy(
            src_ref=lagged.at[step, 1 - core], dst_ref=near.at[step],
            send_sem=near_send.at[step], recv_sem=near_recv.at[step],
            device_id=(me, other_core), device_id_type=MESH,
        )

    def to_chip(step):
        return pltpu.make_async_remote_copy(
            src_ref=joined.at[step], dst_ref=heard.at[step],
            send_sem=sum_send.at[step], recv_sem=sum_recv.at[step],
            device_id=(me, other_chip), device_id_type=MESH,
        )

    for load in loads[:-1]:
        load.wait()
    for load in record_loads[1:] + loads[-1:]:
        load.start()
    pl.semaphore_wait(barrier, 5)

    def whiten_chunk(chunk, carry):
        start = pl.multiple_of(chunk * rows, rows)
        at = pl.ds(start, rows)
        real_part = spectra[at, :BAND]
        imag_part = spectra[at, BAND:]
        amplitude = jnp.sqrt(real_part * real_part + imag_part * imag_part)
        high = amplitude.astype(jnp.bfloat16)
        low = (amplitude - high.astype(jnp.float32)).astype(jnp.bfloat16)
        smooth = jnp.dot(
            jnp.concatenate([high, low], axis=0), inside[...], preferred_element_type=jnp.float32
        )
        smooth = smooth[:rows] + smooth[rows:]
        row = lax.broadcasted_iota(jnp.int32, (rows, channels), 0)
        lane = lax.broadcasted_iota(jnp.int32, (rows, channels), 1)
        picked = jnp.where(lane == chunk * GROUP + row // windows, live_channels[...], 0)
        live = jnp.sum(picked.astype(jnp.float32), axis=1, keepdims=True)
        row = lax.broadcasted_iota(jnp.int32, (rows, windows), 0)
        lane = lax.broadcasted_iota(jnp.int32, (rows, windows), 1)
        picked = jnp.where(lane == row % windows, live_windows[...], 0)
        live = live * jnp.sum(picked.astype(jnp.float32), axis=1, keepdims=True)
        factor = live / (smooth * weight[...] + 1e-06)
        for tile in range(tiles):
            lanes = slice(tile * LANES, (tile + 1) * LANES)
            real = (real_part[:, lanes] * factor[:, lanes]).astype(jnp.bfloat16).astype(jnp.float32)
            imag = (imag_part[:, lanes] * factor[:, lanes]).astype(jnp.bfloat16).astype(jnp.float32)
            for kind, value in enumerate((real, imag, real - imag, real + imag)):
                own[kind, tile, at, :] = value
        for tile in range(tiles):
            for kind in range(2):
                for pair in range(windows // 2):
                    both = [
                        own[kind, tile, pl.ds(start + 2 * pair + part, GROUP, stride=windows), :]
                        for part in range(2)
                    ]
                    own_send[
                        chunk, tile, pl.ds(pair * 2 * GROUP, 2 * GROUP), pl.ds(kind * LANES, LANES)
                    ] = jnp.concatenate(both, axis=0).astype(jnp.bfloat16)
            to_before(chunk, tile).start()

            @pl.when(parity == 1)
            def _():
                to_twin(own_send, chunk, tile).start()

        return carry

    def transform(first, count):
        at = pl.ds(first * rows, count * rows)
        for load in record_loads[first : first + count]:
            load.wait()
        spectra[at, :] = jnp.dot(records[at, :], forward[...], preferred_element_type=jnp.float32)

    transform(0, 1)
    whiten_chunk(0, 0)
    transform(1, chunks - 1)
    lax.fori_loop(1, chunks, whiten_chunk, 0)
    loads[-1].wait()

    def cross_lags(blocks, between):
        count = len(blocks)
        batch = 8 // count
        def tile_step(tile, carry):
            for place, (source, chunk, _) in enumerate(blocks):
                if source is far_two:
                    to_before(chunk, tile).wait_recv()

                    @pl.when(parity == 0)
                    def _():
                        to_twin(far_two, chunk, tile).start()

                else:
                    to_twin(own_send, chunk, tile).wait_recv()
            for place, (source, chunk, _) in enumerate(blocks):
                real = source[chunk, tile, :, :LANES].astype(jnp.float32)
                imag = source[chunk, tile, :, LANES:].astype(jnp.float32)
                far[place, 0] = real + imag
                far[place, 1] = imag
                far[place, 2] = real

            def channel_step(index, inner):
                sums = [[[None] * 3 for _ in range(batch)] for _ in range(count)]
                for window in range(windows):
                    at = pl.ds(window * GROUP, GROUP)
                    far_here = [[far[p, kind, at, :] for kind in range(3)] for p in range(count)]
                    for part in range(batch):
                        base = pl.multiple_of((batch * index + part) * windows, windows)
                        for kind, stored in enumerate((0, 2, 3)):
                            mine = own[stored, tile, pl.ds(base + window, GROUP, stride=0), :]
                            for p in range(count):
                                term = mine * far_here[p][kind]
                                old = sums[p][part][kind]
                                sums[p][part][kind] = term if old is None else old + term
                size = batch * GROUP
                at = pl.ds(pl.multiple_of(index * size, size), size)
                lanes = pl.multiple_of(tile * LANES, LANES)
                for p in range(count):
                    reals = [k[0] - k[1] for k in sums[p]]
                    imags = [k[0] - k[2] for k in sums[p]]
                    cross[p, at, pl.ds(lanes, LANES)] = jnp.concatenate(reals, axis=0).astype(
                        jnp.bfloat16
                    )
                    cross[p, at, pl.ds(BAND + lanes, LANES)] = jnp.concatenate(
                        imags, axis=0
                    ).astype(jnp.bfloat16)
                return inner

            pl.when(tile == 1)(between)
            return lax.fori_loop(0, channels // batch, channel_step, carry)

        lax.fori_loop(0, tiles, tile_step, 0)
        depth = channels * GROUP
        crossed = cross[:count].reshape(count * depth, 2 * BAND)
        result = jnp.dot(crossed, inverse[...], preferred_element_type=jnp.float32) * norm_factor
        for p, (_, _, step) in enumerate(blocks):
            for part in range(n_hour):
                lanes = slice(part * quarter, (part + 1) * quarter)
                lagged[step, part % 2, part // 2] = result[
                    p * depth : (p + 1) * depth, lanes
                ].astype(jnp.bfloat16)
            to_core(step).start()

    def relay(step):
        to_core(step).wait_recv()
        mine = lagged[step, core, 1 - chip].astype(jnp.float32)
        mine = mine + near[step, 1 - chip].astype(jnp.float32)
        joined[step] = mine.astype(jnp.bfloat16)
        to_chip(step).start()

    def finish(chunk, shift):
        step = 2 * chunk + shift
        to_core(step).wait_send()
        to_chip(step).wait()
        value = lagged[step, core, chip].astype(jnp.float32)
        value = value + near[step, chip].astype(jnp.float32) + heard[step].astype(jnp.float32)
        at = pl.ds(pl.multiple_of(chunk * GROUP, GROUP), GROUP)
        total[:, shift, at, :] = value.reshape(channels, GROUP, quarter)

    cross_lags([(far_two, 0, 1)], lambda: None)

    def correlate_chunk(chunk, carry):
        def between():
            relay(2 * chunk + 1)

            @pl.when(chunk >= 1)
            def _():
                relay(2 * chunk - 2)

        cross_lags([(far_two, chunk + 1, 2 * chunk + 3), (far_one, chunk, 2 * chunk)], between)

        @pl.when(chunk >= 1)
        def _():
            finish(chunk - 1, 1)

        @pl.when(chunk >= 2)
        def _():
            finish(chunk - 2, 0)

        return carry

    lax.fori_loop(0, chunks - 1, correlate_chunk, 0)
    last = chunks - 1

    def between_last():
        relay(2 * last + 1)
        relay(2 * last - 2)

    cross_lags([(far_one, last, 2 * last)], between_last)
    relay(2 * last)
    for chunk in range(chunks):
        for tile in range(tiles):
            to_before(chunk, tile).wait_send()
            to_twin(own_send, chunk, tile).wait_send()
    for chunk in range(max(chunks - 2, 0), chunks):
        finish(chunk, 1)
    for chunk in range(max(chunks - 3, 0), chunks):
        finish(chunk, 0)
    out[...] = total[...].astype(jnp.bfloat16)


def local(records, live_channels, live_windows):
    channels, windows, samples = records.shape
    n_chan, n_hour = lax.axis_size("chan"), lax.axis_size("hour")
    norm_factor = 1.0 / math.sqrt(windows * n_hour * BAND)
    chunks, rows, quarter = channels // GROUP, GROUP * windows, LAGS // n_hour
    steps = NSHIFT * chunks
    inside = band_inside()
    weight = (1.0 / inside.sum(axis=0, keepdims=True)).astype(np.float32)
    tiles = BAND // LANES
    whitened = pltpu.VMEM((chunks, tiles, rows, 2 * LANES), jnp.bfloat16)
    return pl.pallas_call(
        functools.partial(kernel, n_chan, n_hour, channels, windows, norm_factor),
        out_shape=jax.ShapeDtypeStruct((channels, NSHIFT, channels, quarter), jnp.bfloat16),
        in_specs=[pl.BlockSpec(memory_space=pltpu.HBM)] * 7,
        out_specs=pl.BlockSpec(memory_space=pltpu.VMEM),
        scratch_shapes=[
            pltpu.VMEM((channels * windows, samples), jnp.bfloat16),
            pltpu.VMEM((1, channels), jnp.int32),
            pltpu.VMEM((1, windows), jnp.int32),
            pltpu.VMEM((SAMPLES, 2 * BAND), jnp.bfloat16),
            pltpu.VMEM((BAND, BAND), jnp.bfloat16),
            pltpu.VMEM((1, BAND), jnp.float32),
            pltpu.VMEM((2 * BAND, LAGS), jnp.bfloat16),
            pltpu.VMEM((channels * windows, 2 * BAND), jnp.float32),
            pltpu.VMEM((4, BAND // LANES, channels * windows, LANES), jnp.float32),
            whitened,
            whitened,
            whitened,
            pltpu.VMEM((NSHIFT, 3, rows, LANES), jnp.float32),
            pltpu.VMEM((NSHIFT, channels * GROUP, 2 * BAND), jnp.bfloat16),
            pltpu.VMEM((steps, 2, n_hour // 2, channels * GROUP, quarter), jnp.bfloat16),
            pltpu.VMEM((steps, n_hour // 2, channels * GROUP, quarter), jnp.bfloat16),
            pltpu.VMEM((steps, channels * GROUP, quarter), jnp.bfloat16),
            pltpu.VMEM((steps, channels * GROUP, quarter), jnp.bfloat16),
            pltpu.VMEM((channels, NSHIFT, channels, quarter), jnp.float32),
            pltpu.SemaphoreType.DMA((6,)),
            pltpu.SemaphoreType.DMA((chunks,)),
            pltpu.SemaphoreType.DMA((chunks, tiles)),
            pltpu.SemaphoreType.DMA((chunks, tiles)),
            pltpu.SemaphoreType.DMA((chunks, tiles)),
            pltpu.SemaphoreType.DMA((chunks, tiles)),
            pltpu.SemaphoreType.DMA((steps,)),
            pltpu.SemaphoreType.DMA((steps,)),
            pltpu.SemaphoreType.DMA((steps,)),
            pltpu.SemaphoreType.DMA((steps,)),
        ],
        compiler_params=pltpu.CompilerParams(
            collective_id=0, has_side_effects=True, vmem_limit_bytes=64 * 1024 * 1024
        ),
        name="correlate",
    )(
        records.reshape(channels * windows, samples),
        live_channels.reshape(1, channels),
        live_windows.reshape(1, windows),
        jnp.asarray(forward_table()),
        jnp.asarray(inside.astype(ml_dtypes.bfloat16)),
        jnp.asarray(weight),
        jnp.asarray(inverse_table()),
    )


def solution(mesh):
    placed = (P("chan", "hour", None), P("chan"), P("hour"))
    return jax.shard_map(
        local, mesh=mesh, in_specs=placed, out_specs=P("chan", None, None, "hour"), check_vma=False
    )
```
